32 devices in a mesh: row: 8 (over z, y), col: 4 (over x, core).
Axes of the slice: x: 2, y: 2, z: 4, core: 2. Of those that a mesh axis runs over, the one named last changes fastest.
Arguments:
- lambda_amps: float32 [32, 32768], P('col', 'row'), may hold values from -6 to 6
- cycle_inter: float32 [32768, 4096], P('row', 'col'), may hold values from -0.03125 to 0.03125
- exchanged: int32 [4096], replicated, may hold values from 0 to 4095, each once
- occ_energy: float32 [64], replicated, may hold values from -1 to -0.25
- virt_energy: float32 [512], replicated, may hold values from 0.25 to 1.5
- row_orbitals: int32 [32, 2], replicated, may hold values from 0 to 63
- col_orbitals: int32 [4096, 2], replicated, may hold values from 0 to 511
Outputs:
- update: float32 [32, 4096], P(('row', 'col'))
The draws below stay inside these ranges and needn't reach their ends.
All inputs are finite; a program needn't handle non-finite values.
Results may differ from the reference program's by a relative error of at most 0.000088.
Values sent between devices are 32-bit elements; how exact they have to be, the bound alone decides.
A program may use at most 64 MiB of HBM per device.

```python
import jax
import jax.numpy as jnp
from jax import lax

OCC = 64
VIRT = 512
PAIRS = 32768
WINDOW = 4096
BRA_ROWS = 32


def set_ends(entries, stream_key, low, largest):
    longest = entries.shape.index(max(entries.shape))
    spots = []
    for shift in (0, 1):
        where = [jax.random.randint(jax.random.fold_in(stream_key, axis), (), 0, length) for axis, length in enumerate(entries.shape)]
        where[longest] = (where[longest] + shift) % entries.shape[longest]
        spots.append(tuple(where))
    return entries.at[spots[0]].set(low).at[spots[1]].set(largest)


def steps_of(stream_key, extent, cuts, low, high):
    factor_of = 1.0
    for position, parts in cuts:
        steps = jax.random.uniform(jax.random.fold_in(jax.random.fold_in(stream_key, 6), position), (parts,), jnp.float32, low / len(cuts), high / len(cuts))
        factor_of = factor_of * jnp.repeat(jnp.exp(steps), extent[position] // parts).reshape((-1,) + (1,) * (len(extent) - 1 - position))
    return factor_of


def normal_values(stream_key, extent, width, reach, cuts=(), kind=jnp.bfloat16):
    result = jax.random.normal(stream_key, extent, jnp.float32) * width
    if len(cuts) > 0:
        result = steps_of(stream_key, extent, cuts, -0.22, 0.18) * result
    return jnp.clip(result, min=-reach, max=reach).astype(kind)


def setup_inputs(seed: int = 0) -> dict:
    key_of = jax.random.split(jax.random.key(seed), 8)
    return {
        "lambda_amps": normal_values(key_of[0], (BRA_ROWS, PAIRS), 1.0, 6.0, ((0, 4), (1, 8)), jnp.float32),
        "cycle_inter": normal_values(key_of[1], (PAIRS, WINDOW), PAIRS ** -0.5, 0.03125, ((0, 8), (1, 4)), jnp.float32),
        "exchanged": jax.random.permutation(key_of[2], WINDOW).astype(jnp.int32),
        "occ_energy": jnp.clip(jax.random.uniform(key_of[3], (OCC,), jnp.float32, -1.0, -0.25), -1.0, -0.25),
        "virt_energy": jnp.clip(jax.random.uniform(key_of[4], (VIRT,), jnp.float32, 0.25, 1.5), 0.25, 1.5),
        "row_orbitals": set_ends(jax.random.randint(key_of[5], (BRA_ROWS, 2), 0, OCC), jax.random.fold_in(key_of[5], 1), 0, OCC - 1).astype(jnp.int32),
        "col_orbitals": set_ends(jax.random.randint(key_of[6], (WINDOW, 2), 0, VIRT), jax.random.fold_in(key_of[6], 1), 0, VIRT - 1).astype(jnp.int32),
    }


def reference(lambda_amps, cycle_inter, exchanged, occ_energy, virt_energy, row_orbitals, col_orbitals):
    cycle = jnp.dot(lambda_amps, cycle_inter, precision=lax.Precision.HIGHEST, preferred_element_type=jnp.float32)
    anti = cycle - jnp.take(cycle, exchanged, axis=1)
    row_part = jnp.take(occ_energy, row_orbitals[:, 0]) + jnp.take(occ_energy, row_orbitals[:, 1])
    col_part = jnp.take(virt_energy, col_orbitals[:, 0]) + jnp.take(virt_energy, col_orbitals[:, 1])
    denom = row_part[:, None] - col_part[None, :]
    return anti / denom
```

```python
import functools

import jax
import jax.numpy as jnp
from jax import lax
from jax.experimental import pallas as pl
from jax.experimental.pallas import tpu as pltpu
from jax.sharding import PartitionSpec as P

MESH = pl.DeviceIdType.MESH
LANES = 128
CHUNKS = 8
TILE = 256


def split(value):
    high = value.astype(jnp.bfloat16)
    low = (value - high.astype(jnp.float32)).astype(jnp.bfloat16)
    return high, low


def look_up(table, index):
    row, lane = index // LANES, index % LANES
    found = jnp.zeros(index.shape, table.dtype)
    for t in range(table.shape[0]):
        spread = jnp.broadcast_to(table[t : t + 1, :], index.shape)
        here = jnp.take_along_axis(spread, lane, axis=1, mode="promise_in_bounds")
        found = jnp.where(row == t, here, found)
    return found


def kernel(
    n_row, n_col,
    lam_hbm, inter_hbm, exch_hbm, occ_hbm, virt_hbm, rows_hbm, cols_hbm, out_ref,
    lam, inter, acc, stage, recv, cyc, exch, occ, virt, rows, cols, pair,
    small_sem, own_sem, inter_sem, lam_send, lam_recv, tile_send, tile_recv,
):
    n_dev = n_row * n_col
    my_row, my_col = lax.axis_index("row"), lax.axis_index("col")
    me = my_row * n_col + my_col
    held, depth = lam_hbm.shape
    step = depth // CHUNKS
    width = inter_hbm.shape[1]
    bra = lam.shape[0]
    blocks = width // LANES

    def inter_copy(k):
        return pltpu.make_async_copy(
            inter_hbm.at[pl.ds(pl.multiple_of(k * step, step), step), :], inter.at[k], inter_sem.at[k]
        )

    for k in range(CHUNKS):
        inter_copy(k).start()

    barrier = pltpu.get_barrier_semaphore()

    def greet(k, carry):
        to = lax.rem(me + k, n_dev)
        pl.semaphore_signal(
            barrier, inc=1, device_id=(to // n_col, lax.rem(to, n_col)), device_id_type=MESH
        )
        return carry

    lax.fori_loop(1, n_dev, greet, 0)

    my_rows = pl.ds(pl.multiple_of(my_col * held, held), held)
    own = pltpu.make_async_copy(lam_hbm, lam.at[my_rows, :], own_sem)
    own.start()
    small = [
        pltpu.make_async_copy(src, dst, small_sem.at[s])
        for s, (src, dst) in enumerate(
            [(exch_hbm, exch), (occ_hbm, occ), (virt_hbm, virt), (rows_hbm, rows), (cols_hbm, cols)]
        )
    ]
    for copy in small:
        copy.start()
    pl.semaphore_wait(barrier, n_dev - 1)

    def push(k, carry):
        part = pl.ds(pl.multiple_of(k * step, step), step)
        for d in range(1, n_col):
            pltpu.make_async_remote_copy(
                src_ref=lam_hbm.at[:, part],
                dst_ref=lam.at[my_rows, part],
                send_sem=lam_send,
                recv_sem=lam_recv.at[k],
                device_id=(my_row, lax.rem(my_col + d, n_col)),
                device_id_type=MESH,
            ).start()
        return carry

    lax.fori_loop(0, CHUNKS, push, 0)
    own.wait()
    others = pl.ds(0, (n_col - 1) * held)
    acc[...] = jnp.zeros_like(acc)

    def multiply(k, carry):
        part = pl.ds(pl.multiple_of(k * step, step), step)
        arrived = lam.at[others, part]
        pltpu.make_async_copy(arrived, arrived, lam_recv.at[k]).wait()
        inter_copy(k).wait()
        high, low = split(lam[:, part])
        both = jnp.concatenate([high, low], axis=0)
        for c in range(0, width, TILE):
            at = slice(c, c + TILE)
            inter_high, inter_low = split(inter[k, :, at])
            first = jnp.dot(both, inter_high, preferred_element_type=jnp.float32)
            second = jnp.dot(high, inter_low, preferred_element_type=jnp.float32)
            acc[:, at] += first[:bra] + (first[bra:] + second)
        return carry

    lax.fori_loop(0, CHUNKS, multiply, 0)

    for b in range(blocks):
        stage[:, b, :] = acc[:, b * LANES : (b + 1) * LANES]

    def scatter(k, carry):
        to = lax.rem(me + k, n_dev)
        pltpu.make_async_remote_copy(
            src_ref=stage.at[to],
            dst_ref=recv.at[me],
            send_sem=tile_send,
            recv_sem=tile_recv,
            device_id=(to // n_col, lax.rem(to, n_col)),
            device_id_type=MESH,
        ).start()
        return carry

    lax.fori_loop(1, n_dev, scatter, 0)
    recv[me] = stage[me]

    for copy in small:
        copy.wait()
    lines = cyc.shape[0]
    for q in range(lines):
        for s in range(2):
            pair[s, q : q + 1, :] = cols[s : s + 1, q * LANES : (q + 1) * LANES]
    col_part = look_up(virt[...], pair[0]) + look_up(virt[...], pair[1])
    orbital = jnp.sum(
        jnp.where(lax.broadcasted_iota(jnp.int32, rows.shape, 1) == me, rows[...], 0), axis=1, keepdims=True
    )
    spread = (2, occ.shape[1])
    picked = jnp.sum(
        jnp.where(
            lax.broadcasted_iota(jnp.int32, spread, 1) == orbital, jnp.broadcast_to(occ[...], spread), 0.0
        ),
        axis=1,
        keepdims=True,
    )
    row_part = picked[0:1] + picked[1:2]
    denom = row_part - col_part
    index = exch[...]

    rest = recv.at[pl.ds(0, n_dev - 1)]
    pltpu.make_async_copy(rest, rest, tile_recv).wait()
    total = recv[pl.ds(0, n_col)]
    for i in range(1, n_row):
        total = total + recv[pl.ds(i * n_col, n_col)]
    for j in range(n_col):
        cyc[j * blocks : (j + 1) * blocks, :] = total[j]
    cycle = cyc[...]
    out_ref[...] = (cycle - look_up(cycle, index)) / denom

    sent = stage.at[pl.ds(0, n_dev - 1)]
    pltpu.make_async_copy(sent, sent, tile_send).wait()
    gone = lam.at[others, :]
    pltpu.make_async_copy(gone, gone, lam_send).wait()


def shards(
    lambda_amps, cycle_inter, exchanged, occ_energy, virt_energy, row_orbitals, col_orbitals
):
    n_row, n_col = lax.axis_size("row"), lax.axis_size("col")
    n_dev = n_row * n_col
    held, depth = lambda_amps.shape
    width = cycle_inter.shape[1]
    bra = held * n_col
    window = exchanged.shape[0]
    assert bra == n_dev
    blocks, lines = width // LANES, window // LANES
    f32, i32 = jnp.float32, jnp.int32
    small = [
        exchanged.reshape(lines, LANES),
        occ_energy.reshape(1, -1),
        virt_energy.reshape(-1, LANES),
        row_orbitals.T,
        col_orbitals.T,
    ]
    out = pl.pallas_call(
        functools.partial(kernel, n_row, n_col),
        out_shape=jax.ShapeDtypeStruct((lines, LANES), f32),
        in_specs=[pl.BlockSpec(memory_space=pl.ANY)] * 7,
        out_specs=pl.BlockSpec(memory_space=pltpu.VMEM),
        scratch_shapes=[
            pltpu.VMEM((bra, depth), f32),
            pltpu.VMEM((CHUNKS, depth // CHUNKS, width), f32),
            pltpu.VMEM((bra, width), f32),
            pltpu.VMEM((n_dev, blocks, LANES), f32),
            pltpu.VMEM((n_dev, blocks, LANES), f32),
            pltpu.VMEM((lines, LANES), f32),
            *[pltpu.VMEM(x.shape, x.dtype) for x in small],
            pltpu.VMEM((2, lines, LANES), i32),
            pltpu.SemaphoreType.DMA((5,)),
            pltpu.SemaphoreType.DMA,
            pltpu.SemaphoreType.DMA((CHUNKS,)),
            pltpu.SemaphoreType.DMA,
            pltpu.SemaphoreType.DMA((CHUNKS,)),
            pltpu.SemaphoreType.DMA,
            pltpu.SemaphoreType.DMA,
        ],
        compiler_params=pltpu.CompilerParams(
            collective_id=0, has_side_effects=True, vmem_limit_bytes=56 * 2**20
        ),
        cost_estimate=pl.CostEstimate(
            flops=2 * bra * depth * width, bytes_accessed=4 * depth * width, transcendentals=0
        ),
    )(lambda_amps, cycle_inter, *small)
    return out.reshape(1, window)


def solution(mesh):
    placed = (P("col", "row"), P("row", "col"), P(), P(), P(), P(), P())
    return jax.shard_map(
        shards, mesh=mesh, in_specs=placed, out_specs=P(("row", "col"), None), check_vma=False
    )
```

```python
import functools

import jax
import jax.numpy as jnp
from jax import lax
from jax.experimental import pallas as pl
from jax.experimental.pallas import tpu as pltpu
from jax.sharding import PartitionSpec as P

MESH = pl.DeviceIdType.MESH
LANES = 128
CHUNKS = 8
AHEAD = 2
TILE = 256


def split(value):
    high = value.astype(jnp.bfloat16)
    low = (value - high.astype(jnp.float32)).astype(jnp.bfloat16)
    return high, low


def look_up(table, index):
    row, lane = index // LANES, index % LANES
    found = jnp.zeros(index.shape, table.dtype)
    for t in range(table.shape[0]):
        spread = jnp.broadcast_to(table[t : t + 1, :], index.shape)
        here = jnp.take_along_axis(spread, lane, axis=1, mode="promise_in_bounds")
        found = jnp.where(row == t, here, found)
    return found


def kernel(
    n_row, n_col,
    lam_hbm, inter_hbm, exch_hbm, occ_hbm, virt_hbm, rows_hbm, cols_hbm, anti_ref, denom_ref,
    lam, inter, acc, stage, recv, cyc, exch, occ, virt, rows, cols, pair,
    small_sem, own_sem, inter_sem, near_send, near_recv, far_send, far_recv, relay_send, relay_recv,
    tile_send, tile_recv,
):
    n_dev = n_row * n_col
    my_row, my_col = lax.axis_index("row"), lax.axis_index("col")
    me = my_row * n_col + my_col
    held, depth = lam_hbm.shape
    step = depth // CHUNKS
    width = inter_hbm.shape[1]
    bra = lam.shape[0]
    blocks = width // LANES

    def inter_copy(k):
        return pltpu.make_async_copy(
            inter_hbm.at[pl.ds(pl.multiple_of(k * step, step), step), :], inter.at[k], inter_sem.at[k]
        )

    for k in range(CHUNKS):
        inter_copy(k).start()

    barrier = pltpu.get_barrier_semaphore()

    def greet(k, carry):
        to = lax.rem(me + k, n_dev)
        pl.semaphore_signal(
            barrier, inc=1, device_id=(to // n_col, lax.rem(to, n_col)), device_id_type=MESH
        )
        return carry

    lax.fori_loop(1, n_dev, greet, 0)

    my_rows = pl.ds(pl.multiple_of(my_col * held, held), held)
    own = pltpu.make_async_copy(lam_hbm, lam.at[my_rows, :], own_sem)
    own.start()
    small = [
        pltpu.make_async_copy(src, dst, small_sem.at[s])
        for s, (src, dst) in enumerate(
            [(exch_hbm, exch), (occ_hbm, occ), (virt_hbm, virt), (rows_hbm, rows), (cols_hbm, cols)]
        )
    ]
    for copy in small:
        copy.start()
    pl.semaphore_wait(barrier, n_dev - 1)

    def chunk(k):
        return pl.ds(pl.multiple_of(k * step, step), step)

    def rows_of(col):
        return pl.ds(pl.multiple_of(col * held, held), held)

    core = lax.rem(my_col, 2)
    mate = my_col + 1 - 2 * core
    n_far = n_col // 2 - 1
    peers = [lax.rem(my_col + 2 * d, n_col) for d in range(1, n_far + 1)]

    def push(k, carry):
        for peer in peers:
            pltpu.make_async_remote_copy(
                src_ref=lam_hbm.at[:, chunk(k)],
                dst_ref=lam.at[my_rows, chunk(k)],
                send_sem=far_send,
                recv_sem=far_recv.at[k],
                device_id=(my_row, peer),
                device_id_type=MESH,
            ).start()
        return carry

    def forward(k):
        arrived = lam.at[pl.ds(0, n_far * held), chunk(k)]
        pltpu.make_async_copy(arrived, arrived, far_recv.at[k]).wait()
        for peer in peers:
            pltpu.make_async_remote_copy(
                src_ref=lam.at[rows_of(peer), chunk(k)],
                dst_ref=lam.at[rows_of(peer), chunk(k)],
                send_sem=relay_send,
                recv_sem=relay_recv.at[k],
                device_id=(my_row, mate),
                device_id_type=MESH,
            ).start()

    lax.fori_loop(0, CHUNKS, push, 0)
    near = pltpu.make_async_remote_copy(
        src_ref=lam_hbm,
        dst_ref=lam.at[my_rows, :],
        send_sem=near_send,
        recv_sem=near_recv,
        device_id=(my_row, mate),
        device_id_type=MESH,
    )
    near.start()
    for k in range(AHEAD):
        forward(k)
    near.wait_recv()
    own.wait()
    acc[...] = jnp.zeros_like(acc)

    def multiply(k, carry):
        @pl.when(k + AHEAD < CHUNKS)
        def _():
            forward(k + AHEAD)

        arrived = lam.at[pl.ds(0, n_far * held), chunk(k)]
        pltpu.make_async_copy(arrived, arrived, relay_recv.at[k]).wait()
        inter_copy(k).wait()
        high, low = split(lam[:, chunk(k)])
        both = jnp.concatenate([high, low], axis=0)
        for c in range(0, width, TILE):
            at = slice(c, c + TILE)
            inter_high, inter_low = split(inter[k, :, at])
            first = jnp.dot(both, inter_high, preferred_element_type=jnp.float32)
            second = jnp.dot(high, inter_low, preferred_element_type=jnp.float32)
            acc[:, at] += first[:bra] + (first[bra:] + second)
        return carry

    lax.fori_loop(0, CHUNKS, multiply, 0)

    for b in range(blocks):
        stage[:, b, :] = acc[:, b * LANES : (b + 1) * LANES]

    def scatter(k, carry):
        to = lax.rem(me + k, n_dev)
        pltpu.make_async_remote_copy(
            src_ref=stage.at[to],
            dst_ref=recv.at[me],
            send_sem=tile_send,
            recv_sem=tile_recv,
            device_id=(to // n_col, lax.rem(to, n_col)),
            device_id_type=MESH,
        ).start()
        return carry

    lax.fori_loop(1, n_dev, scatter, 0)
    recv[me] = stage[me]

    for copy in small:
        copy.wait()
    lines = cyc.shape[0]
    for q in range(lines):
        for s in range(2):
            pair[s, q : q + 1, :] = cols[s : s + 1, q * LANES : (q + 1) * LANES]
    col_part = look_up(virt[...], pair[0]) + look_up(virt[...], pair[1])
    orbital = jnp.sum(
        jnp.where(lax.broadcasted_iota(jnp.int32, rows.shape, 1) == me, rows[...], 0), axis=1, keepdims=True
    )
    spread = (2, occ.shape[1])
    picked = jnp.sum(
        jnp.where(
            lax.broadcasted_iota(jnp.int32, spread, 1) == orbital, jnp.broadcast_to(occ[...], spread), 0.0
        ),
        axis=1,
        keepdims=True,
    )
    row_part = picked[0:1] + picked[1:2]
    denom_ref[...] = row_part - col_part
    index = exch[...]

    rest = recv.at[pl.ds(0, n_dev - 1)]
    pltpu.make_async_copy(rest, rest, tile_recv).wait()
    total = recv[pl.ds(0, n_col)]
    for i in range(1, n_row):
        total = total + recv[pl.ds(i * n_col, n_col)]
    for j in range(n_col):
        cyc[j * blocks : (j + 1) * blocks, :] = total[j]
    cycle = cyc[...]
    anti_ref[...] = cycle - look_up(cycle, index)

    sent = stage.at[pl.ds(0, n_dev - 1)]
    pltpu.make_async_copy(sent, sent, tile_send).wait()
    near.wait_send()
    gone = lam.at[pl.ds(0, n_far * held), :]
    pltpu.make_async_copy(gone, gone, far_send).wait()
    pltpu.make_async_copy(gone, gone, relay_send).wait()


def shards(
    lambda_amps, cycle_inter, exchanged, occ_energy, virt_energy, row_orbitals, col_orbitals
):
    n_row, n_col = lax.axis_size("row"), lax.axis_size("col")
    n_dev = n_row * n_col
    held, depth = lambda_amps.shape
    width = cycle_inter.shape[1]
    bra = held * n_col
    window = exchanged.shape[0]
    assert bra == n_dev and n_col % 2 == 0 and n_col > 2
    blocks, lines = width // LANES, window // LANES
    f32, i32 = jnp.float32, jnp.int32
    small = [
        exchanged.reshape(lines, LANES),
        occ_energy.reshape(1, -1),
        virt_energy.reshape(-1, LANES),
        row_orbitals.T,
        col_orbitals.T,
    ]
    line = jax.ShapeDtypeStruct((lines, LANES), f32)
    anti, denom = pl.pallas_call(
        functools.partial(kernel, n_row, n_col),
        out_shape=(line, line),
        in_specs=[pl.BlockSpec(memory_space=pl.ANY)] * 7,
        out_specs=(pl.BlockSpec(memory_space=pltpu.VMEM),) * 2,
        scratch_shapes=[
            pltpu.VMEM((bra, depth), f32),
            pltpu.VMEM((CHUNKS, depth // CHUNKS, width), f32),
            pltpu.VMEM((bra, width), f32),
            pltpu.VMEM((n_dev, blocks, LANES), f32),
            pltpu.VMEM((n_dev, blocks, LANES), f32),
            pltpu.VMEM((lines, LANES), f32),
            *[pltpu.VMEM(x.shape, x.dtype) for x in small],
            pltpu.VMEM((2, lines, LANES), i32),
            pltpu.SemaphoreType.DMA((5,)),
            pltpu.SemaphoreType.DMA,
            pltpu.SemaphoreType.DMA((CHUNKS,)),
            pltpu.SemaphoreType.DMA,
            pltpu.SemaphoreType.DMA,
            pltpu.SemaphoreType.DMA,
            pltpu.SemaphoreType.DMA((CHUNKS,)),
            pltpu.SemaphoreType.DMA,
            pltpu.SemaphoreType.DMA((CHUNKS,)),
            pltpu.SemaphoreType.DMA,
            pltpu.SemaphoreType.DMA,
        ],
        compiler_params=pltpu.CompilerParams(
            collective_id=0, has_side_effects=True, vmem_limit_bytes=56 * 2**20
        ),
        cost_estimate=pl.CostEstimate(
            flops=2 * bra * depth * width, bytes_accessed=4 * depth * width, transcendentals=0
        ),
    )(lambda_amps, cycle_inter, *small)
    return (anti / denom).reshape(1, window)


def solution(mesh):
    placed = (P("col", "row"), P("row", "col"), P(), P(), P(), P(), P())
    return jax.shard_map(
        shards, mesh=mesh, in_specs=placed, out_specs=P(("row", "col"), None), check_vma=False
    )
```

```python
import functools

import jax
import jax.numpy as jnp
from jax import lax
from jax.experimental import pallas as pl
from jax.experimental.pallas import tpu as pltpu
from jax.sharding import PartitionSpec as P

MESH = pl.DeviceIdType.MESH
LANES = 128
CHUNKS = 8
AHEAD = 2
TILE = 256


def split(value):
    high = value.astype(jnp.bfloat16)
    low = (value - high.astype(jnp.float32)).astype(jnp.bfloat16)
    return high, low


def look_up(table, index):
    row, lane = index // LANES, index % LANES
    found = jnp.zeros(index.shape, table.dtype)
    for t in range(table.shape[0]):
        spread = jnp.broadcast_to(table[t : t + 1, :], index.shape)
        here = jnp.take_along_axis(spread, lane, axis=1, mode="promise_in_bounds")
        found = jnp.where(row == t, here, found)
    return found


def kernel(
    n_row, n_col,
    lam_hbm, inter_hbm, exch_hbm, occ_hbm, virt_hbm, rows_hbm, cols_hbm, anti_ref, denom_ref,
    lam, inter, even_high, even_low, odd_high, odd_low, acc, stage, recv, cyc, exch, occ, virt, rows, cols, pair,
    small_sem, own_sem, inter_sem, near_send, near_recv, far_send, far_recv, relay_send, relay_recv,
    tile_send, tile_recv,
):
    n_dev = n_row * n_col
    even, odd = (even_high, even_low), (odd_high, odd_low)
    my_row, my_col = lax.axis_index("row"), lax.axis_index("col")
    me = my_row * n_col + my_col
    held, depth = lam_hbm.shape
    step = depth // CHUNKS
    width = inter_hbm.shape[1]
    bra = lam.shape[0]
    blocks = width // LANES

    def inter_copy(k):
        return pltpu.make_async_copy(
            inter_hbm.at[pl.ds(pl.multiple_of(k * step, step), step), :], inter.at[k], inter_sem.at[k]
        )

    for k in range(CHUNKS):
        inter_copy(k).start()

    barrier = pltpu.get_barrier_semaphore()

    def greet(k, carry):
        to = lax.rem(me + k, n_dev)
        pl.semaphore_signal(
            barrier, inc=1, device_id=(to // n_col, lax.rem(to, n_col)), device_id_type=MESH
        )
        return carry

    lax.fori_loop(1, n_dev, greet, 0)

    my_rows = pl.ds(pl.multiple_of(my_col * held, held), held)
    own = pltpu.make_async_copy(lam_hbm, lam.at[my_rows, :], own_sem)
    own.start()
    small = [
        pltpu.make_async_copy(src, dst, small_sem.at[s])
        for s, (src, dst) in enumerate(
            [(exch_hbm, exch), (occ_hbm, occ), (virt_hbm, virt), (rows_hbm, rows), (cols_hbm, cols)]
        )
    ]
    for copy in small:
        copy.start()
    pl.semaphore_wait(barrier, n_dev - 1)

    def chunk(k):
        return pl.ds(pl.multiple_of(k * step, step), step)

    def rows_of(col):
        return pl.ds(pl.multiple_of(col * held, held), held)

    core = lax.rem(my_col, 2)
    mate = my_col + 1 - 2 * core
    n_far = n_col // 2 - 1
    peers = [lax.rem(my_col + 2 * d, n_col) for d in range(1, n_far + 1)]

    def push(k, carry):
        for peer in peers:
            pltpu.make_async_remote_copy(
                src_ref=lam_hbm.at[:, chunk(k)],
                dst_ref=lam.at[my_rows, chunk(k)],
                send_sem=far_send,
                recv_sem=far_recv.at[k],
                device_id=(my_row, peer),
                device_id_type=MESH,
            ).start()
        return carry

    def forward(k):
        arrived = lam.at[pl.ds(0, n_far * held), chunk(k)]
        pltpu.make_async_copy(arrived, arrived, far_recv.at[k]).wait()
        for peer in peers:
            pltpu.make_async_remote_copy(
                src_ref=lam.at[rows_of(peer), chunk(k)],
                dst_ref=lam.at[rows_of(peer), chunk(k)],
                send_sem=relay_send,
                recv_sem=relay_recv.at[k],
                device_id=(my_row, mate),
                device_id_type=MESH,
            ).start()

    lax.fori_loop(0, CHUNKS, push, 0)
    near = pltpu.make_async_remote_copy(
        src_ref=lam_hbm,
        dst_ref=lam.at[my_rows, :],
        send_sem=near_send,
        recv_sem=near_recv,
        device_id=(my_row, mate),
        device_id_type=MESH,
    )
    near.start()
    acc[...] = jnp.zeros_like(acc)

    tiles = [(r, c) for c in range(0, width, TILE) for r in range(0, step, TILE)]

    def convert(k, part, r, c):
        at = (slice(r, r + TILE), slice(c, c + TILE))
        part[0][at], part[1][at] = split(inter[k, at[0], at[1]])

    def multiply(k, ready, filling):
        @pl.when(k + AHEAD < CHUNKS)
        def _():
            forward(k + AHEAD)

        @pl.when(k + 1 < CHUNKS)
        def _():
            inter_copy(k + 1).wait()

        arrived = lam.at[pl.ds(0, n_far * held), chunk(k)]
        pltpu.make_async_copy(arrived, arrived, relay_recv.at[k]).wait()
        after = jnp.minimum(k + 1, CHUNKS - 1)
        high, low = split(lam[:, chunk(k)])
        both = jnp.concatenate([high, low], axis=0)
        for r, c in tiles:
            convert(after, filling, r, c)
            rows_at, at = slice(r, r + TILE), slice(c, c + TILE)
            first = jnp.dot(both[:, rows_at], ready[0][rows_at, at], preferred_element_type=jnp.float32)
            second = jnp.dot(high[:, rows_at], ready[1][rows_at, at], preferred_element_type=jnp.float32)
            acc[:, at] += first[:bra] + (first[bra:] + second)

    inter_copy(0).wait()
    for r, c in tiles:
        convert(0, even, r, c)
    for k in range(AHEAD):
        forward(k)
    near.wait_recv()
    own.wait()

    def twice(t, carry):
        multiply(2 * t, even, odd)
        multiply(2 * t + 1, odd, even)
        return carry

    lax.fori_loop(0, CHUNKS // 2, twice, 0)

    for b in range(blocks):
        stage[:, b, :] = acc[:, b * LANES : (b + 1) * LANES]

    def scatter(k, carry):
        to = lax.rem(me + k, n_dev)
        pltpu.make_async_remote_copy(
            src_ref=stage.at[to],
            dst_ref=recv.at[me],
            send_sem=tile_send,
            recv_sem=tile_recv,
            device_id=(to // n_col, lax.rem(to, n_col)),
            device_id_type=MESH,
        ).start()
        return carry

    lax.fori_loop(1, n_dev, scatter, 0)
    recv[me] = stage[me]

    for copy in small:
        copy.wait()
    lines = cyc.shape[0]
    for q in range(lines):
        for s in range(2):
            pair[s, q : q + 1, :] = cols[s : s + 1, q * LANES : (q + 1) * LANES]
    col_part = look_up(virt[...], pair[0]) + look_up(virt[...], pair[1])
    orbital = jnp.sum(
        jnp.where(lax.broadcasted_iota(jnp.int32, rows.shape, 1) == me, rows[...], 0), axis=1, keepdims=True
    )
    spread = (2, occ.shape[1])
    picked = jnp.sum(
        jnp.where(
            lax.broadcasted_iota(jnp.int32, spread, 1) == orbital, jnp.broadcast_to(occ[...], spread), 0.0
        ),
        axis=1,
        keepdims=True,
    )
    row_part = picked[0:1] + picked[1:2]
    denom_ref[...] = row_part - col_part
    index = exch[...]

    rest = recv.at[pl.ds(0, n_dev - 1)]
    pltpu.make_async_copy(rest, rest, tile_recv).wait()
    total = recv[pl.ds(0, n_col)]
    for i in range(1, n_row):
        total = total + recv[pl.ds(i * n_col, n_col)]
    for j in range(n_col):
        cyc[j * blocks : (j + 1) * blocks, :] = total[j]
    cycle = cyc[...]
    anti_ref[...] = cycle - look_up(cycle, index)

    sent = stage.at[pl.ds(0, n_dev - 1)]
    pltpu.make_async_copy(sent, sent, tile_send).wait()
    near.wait_send()
    gone = lam.at[pl.ds(0, n_far * held), :]
    pltpu.make_async_copy(gone, gone, far_send).wait()
    pltpu.make_async_copy(gone, gone, relay_send).wait()


def shards(
    lambda_amps, cycle_inter, exchanged, occ_energy, virt_energy, row_orbitals, col_orbitals
):
    n_row, n_col = lax.axis_size("row"), lax.axis_size("col")
    n_dev = n_row * n_col
    held, depth = lambda_amps.shape
    width = cycle_inter.shape[1]
    bra = held * n_col
    window = exchanged.shape[0]
    assert bra == n_dev and n_col % 2 == 0 and n_col > 2
    blocks, lines = width // LANES, window // LANES
    f32, i32 = jnp.float32, jnp.int32
    small = [
        exchanged.reshape(lines, LANES),
        occ_energy.reshape(1, -1),
        virt_energy.reshape(-1, LANES),
        row_orbitals.T,
        col_orbitals.T,
    ]
    line = jax.ShapeDtypeStruct((lines, LANES), f32)
    anti, denom = pl.pallas_call(
        functools.partial(kernel, n_row, n_col),
        out_shape=(line, line),
        in_specs=[pl.BlockSpec(memory_space=pl.ANY)] * 7,
        out_specs=(pl.BlockSpec(memory_space=pltpu.VMEM),) * 2,
        scratch_shapes=[
            pltpu.VMEM((bra, depth), f32),
            pltpu.VMEM((CHUNKS, depth // CHUNKS, width), f32),
            *[pltpu.VMEM((depth // CHUNKS, width), jnp.bfloat16)] * 4,
            pltpu.VMEM((bra, width), f32),
            pltpu.VMEM((n_dev, blocks, LANES), f32),
            pltpu.VMEM((n_dev, blocks, LANES), f32),
            pltpu.VMEM((lines, LANES), f32),
            *[pltpu.VMEM(x.shape, x.dtype) for x in small],
            pltpu.VMEM((2, lines, LANES), i32),
            pltpu.SemaphoreType.DMA((5,)),
            pltpu.SemaphoreType.DMA,
            pltpu.SemaphoreType.DMA((CHUNKS,)),
            pltpu.SemaphoreType.DMA,
            pltpu.SemaphoreType.DMA,
            pltpu.SemaphoreType.DMA,
            pltpu.SemaphoreType.DMA((CHUNKS,)),
            pltpu.SemaphoreType.DMA,
            pltpu.SemaphoreType.DMA((CHUNKS,)),
            pltpu.SemaphoreType.DMA,
            pltpu.SemaphoreType.DMA,
        ],
        compiler_params=pltpu.CompilerParams(
            collective_id=0, has_side_effects=True, vmem_limit_bytes=56 * 2**20
        ),
        cost_estimate=pl.CostEstimate(
            flops=2 * bra * depth * width, bytes_accessed=4 * depth * width, transcendentals=0
        ),
    )(lambda_amps, cycle_inter, *small)
    return (anti / denom).reshape(1, window)


def solution(mesh):
    placed = (P("col", "row"), P("row", "col"), P(), P(), P(), P(), P())
    return jax.shard_map(
        shards, mesh=mesh, in_specs=placed, out_specs=P(("row", "col"), None), check_vma=False
    )
```

```python
import functools

import jax
import jax.numpy as jnp
from jax import lax
from jax.experimental import pallas as pl
from jax.experimental.pallas import tpu as pltpu
from jax.sharding import PartitionSpec as P

MESH = pl.DeviceIdType.MESH
LANES = 128
CHUNKS = 4
AHEAD = 1
TILE = 256


def split(value):
    high = value.astype(jnp.bfloat16)
    low = (value - high.astype(jnp.float32)).astype(jnp.bfloat16)
    return high, low


def look_up(table, index):
    row, lane = index // LANES, index % LANES
    found = jnp.zeros(index.shape, table.dtype)
    for t in range(table.shape[0]):
        spread = jnp.broadcast_to(table[t : t + 1, :], index.shape)
        here = jnp.take_along_axis(spread, lane, axis=1, mode="promise_in_bounds")
        found = jnp.where(row == t, here, found)
    return found


def kernel(
    n_row, n_col,
    lam_hbm, inter_hbm, exch_hbm, occ_hbm, virt_hbm, rows_hbm, cols_hbm, anti_ref, denom_ref,
    lam, inter, acc, stage, recv, cyc, exch, occ, virt, rows, cols, pair,
    small_sem, own_sem, inter_sem, near_send, near_recv, far_send, far_recv, relay_send, relay_recv,
    tile_send, tile_recv,
):
    n_dev = n_row * n_col
    my_row, my_col = lax.axis_index("row"), lax.axis_index("col")
    me = my_row * n_col + my_col
    held, depth = lam_hbm.shape
    step = depth // CHUNKS
    width = inter_hbm.shape[1]
    bra = lam.shape[0]
    blocks = width // LANES

    def inter_copy(k):
        return pltpu.make_async_copy(
            inter_hbm.at[pl.ds(pl.multiple_of(k * step, step), step), :], inter.at[k], inter_sem.at[k]
        )

    for k in range(CHUNKS):
        inter_copy(k).start()

    barrier = pltpu.get_barrier_semaphore()

    def greet(k, carry):
        to = lax.rem(me + k, n_dev)
        pl.semaphore_signal(
            barrier, inc=1, device_id=(to // n_col, lax.rem(to, n_col)), device_id_type=MESH
        )
        return carry

    lax.fori_loop(1, n_dev, greet, 0)

    my_rows = pl.ds(pl.multiple_of(my_col * held, held), held)
    own = pltpu.make_async_copy(lam_hbm, lam.at[my_rows, :], own_sem)
    own.start()
    small = [
        pltpu.make_async_copy(src, dst, small_sem.at[s])
        for s, (src, dst) in enumerate(
            [(exch_hbm, exch), (occ_hbm, occ), (virt_hbm, virt), (rows_hbm, rows), (cols_hbm, cols)]
        )
    ]
    for copy in small:
        copy.start()
    pl.semaphore_wait(barrier, n_dev - 1)

    def chunk(k):
        return pl.ds(pl.multiple_of(k * step, step), step)

    def rows_of(col):
        return pl.ds(pl.multiple_of(col * held, held), held)

    core = lax.rem(my_col, 2)
    mate = my_col + 1 - 2 * core
    n_far = n_col // 2 - 1
    peers = [lax.rem(my_col + 2 * d, n_col) for d in range(1, n_far + 1)]

    def push(k, carry):
        for peer in peers:
            pltpu.make_async_remote_copy(
                src_ref=lam_hbm.at[:, chunk(k)],
                dst_ref=lam.at[my_rows, chunk(k)],
                send_sem=far_send,
                recv_sem=far_recv.at[k],
                device_id=(my_row, peer),
                device_id_type=MESH,
            ).start()
        return carry

    def forward(k):
        arrived = lam.at[pl.ds(0, n_far * held), chunk(k)]
        pltpu.make_async_copy(arrived, arrived, far_recv.at[k]).wait()
        for peer in peers:
            pltpu.make_async_remote_copy(
                src_ref=lam.at[rows_of(peer), chunk(k)],
                dst_ref=lam.at[rows_of(peer), chunk(k)],
                send_sem=relay_send,
                recv_sem=relay_recv.at[k],
                device_id=(my_row, mate),
                device_id_type=MESH,
            ).start()

    lax.fori_loop(0, CHUNKS, push, 0)
    near = pltpu.make_async_remote_copy(
        src_ref=lam_hbm,
        dst_ref=lam.at[my_rows, :],
        send_sem=near_send,
        recv_sem=near_recv,
        device_id=(my_row, mate),
        device_id_type=MESH,
    )
    near.start()
    for k in range(AHEAD):
        forward(k)
    near.wait_recv()
    own.wait()
    acc[...] = jnp.zeros_like(acc)

    def multiply(k, carry):
        @pl.when(k + AHEAD < CHUNKS)
        def _():
            forward(k + AHEAD)

        arrived = lam.at[pl.ds(0, n_far * held), chunk(k)]
        pltpu.make_async_copy(arrived, arrived, relay_recv.at[k]).wait()
        inter_copy(k).wait()
        high, low = split(lam[:, chunk(k)])
        both = jnp.concatenate([high, low], axis=0)
        for c in range(0, width, TILE):
            at = slice(c, c + TILE)
            first = second = 0.0
            for r in range(0, step, TILE):
                rows_at = slice(r, r + TILE)
                inter_high, inter_low = split(inter[k, rows_at, at])
                first += jnp.dot(both[:, rows_at], inter_high, preferred_element_type=jnp.float32)
                second += jnp.dot(high[:, rows_at], inter_low, preferred_element_type=jnp.float32)
            acc[:, at] += first[:bra] + (first[bra:] + second)
        return carry

    lax.fori_loop(0, CHUNKS, multiply, 0)

    for b in range(blocks):
        stage[:, b, :] = acc[:, b * LANES : (b + 1) * LANES]

    def scatter(k, carry):
        to = lax.rem(me + k, n_dev)
        pltpu.make_async_remote_copy(
            src_ref=stage.at[to],
            dst_ref=recv.at[me],
            send_sem=tile_send,
            recv_sem=tile_recv,
            device_id=(to // n_col, lax.rem(to, n_col)),
            device_id_type=MESH,
        ).start()
        return carry

    lax.fori_loop(1, n_dev, scatter, 0)
    recv[me] = stage[me]

    for copy in small:
        copy.wait()
    lines = cyc.shape[0]
    for q in range(lines):
        for s in range(2):
            pair[s, q : q + 1, :] = cols[s : s + 1, q * LANES : (q + 1) * LANES]
    col_part = look_up(virt[...], pair[0]) + look_up(virt[...], pair[1])
    orbital = jnp.sum(
        jnp.where(lax.broadcasted_iota(jnp.int32, rows.shape, 1) == me, rows[...], 0), axis=1, keepdims=True
    )
    spread = (2, occ.shape[1])
    picked = jnp.sum(
        jnp.where(
            lax.broadcasted_iota(jnp.int32, spread, 1) == orbital, jnp.broadcast_to(occ[...], spread), 0.0
        ),
        axis=1,
        keepdims=True,
    )
    row_part = picked[0:1] + picked[1:2]
    denom_ref[...] = row_part - col_part
    index = exch[...]

    rest = recv.at[pl.ds(0, n_dev - 1)]
    pltpu.make_async_copy(rest, rest, tile_recv).wait()
    total = recv[pl.ds(0, n_col)]
    for i in range(1, n_row):
        total = total + recv[pl.ds(i * n_col, n_col)]
    for j in range(n_col):
        cyc[j * blocks : (j + 1) * blocks, :] = total[j]
    cycle = cyc[...]
    anti_ref[...] = cycle - look_up(cycle, index)

    sent = stage.at[pl.ds(0, n_dev - 1)]
    pltpu.make_async_copy(sent, sent, tile_send).wait()
    near.wait_send()
    gone = lam.at[pl.ds(0, n_far * held), :]
    pltpu.make_async_copy(gone, gone, far_send).wait()
    pltpu.make_async_copy(gone, gone, relay_send).wait()


def shards(
    lambda_amps, cycle_inter, exchanged, occ_energy, virt_energy, row_orbitals, col_orbitals
):
    n_row, n_col = lax.axis_size("row"), lax.axis_size("col")
    n_dev = n_row * n_col
    held, depth = lambda_amps.shape
    width = cycle_inter.shape[1]
    bra = held * n_col
    window = exchanged.shape[0]
    assert bra == n_dev and n_col % 2 == 0 and n_col > 2
    blocks, lines = width // LANES, window // LANES
    f32, i32 = jnp.float32, jnp.int32
    small = [
        exchanged.reshape(lines, LANES),
        occ_energy.reshape(1, -1),
        virt_energy.reshape(-1, LANES),
        row_orbitals.T,
        col_orbitals.T,
    ]
    line = jax.ShapeDtypeStruct((lines, LANES), f32)
    anti, denom = pl.pallas_call(
        functools.partial(kernel, n_row, n_col),
        out_shape=(line, line),
        in_specs=[pl.BlockSpec(memory_space=pl.ANY)] * 7,
        out_specs=(pl.BlockSpec(memory_space=pltpu.VMEM),) * 2,
        scratch_shapes=[
            pltpu.VMEM((bra, depth), f32),
            pltpu.VMEM((CHUNKS, depth // CHUNKS, width), f32),
            pltpu.VMEM((bra, width), f32),
            pltpu.VMEM((n_dev, blocks, LANES), f32),
            pltpu.VMEM((n_dev, blocks, LANES), f32),
            pltpu.VMEM((lines, LANES), f32),
            *[pltpu.VMEM(x.shape, x.dtype) for x in small],
            pltpu.VMEM((2, lines, LANES), i32),
            pltpu.SemaphoreType.DMA((5,)),
            pltpu.SemaphoreType.DMA,
            pltpu.SemaphoreType.DMA((CHUNKS,)),
            pltpu.SemaphoreType.DMA,
            pltpu.SemaphoreType.DMA,
            pltpu.SemaphoreType.DMA,
            pltpu.SemaphoreType.DMA((CHUNKS,)),
            pltpu.SemaphoreType.DMA,
            pltpu.SemaphoreType.DMA((CHUNKS,)),
            pltpu.SemaphoreType.DMA,
            pltpu.SemaphoreType.DMA,
        ],
        compiler_params=pltpu.CompilerParams(
            collective_id=0, has_side_effects=True, vmem_limit_bytes=56 * 2**20
        ),
        cost_estimate=pl.CostEstimate(
            flops=2 * bra * depth * width, bytes_accessed=4 * depth * width, transcendentals=0
        ),
    )(lambda_amps, cycle_inter, *small)
    return (anti / denom).reshape(1, window)


def solution(mesh):
    placed = (P("col", "row"), P("row", "col"), P(), P(), P(), P(), P())
    return jax.shard_map(
        shards, mesh=mesh, in_specs=placed, out_specs=P(("row", "col"), None), check_vma=False
    )
```

```python
import functools

import jax
import jax.numpy as jnp
from jax import lax
from jax.experimental import pallas as pl
from jax.experimental.pallas import tpu as pltpu
from jax.sharding import PartitionSpec as P

MESH = pl.DeviceIdType.MESH
LANES = 128
CHUNKS = 4
AHEAD = 1
TILE = 256


def split(value):
    high = value.astype(jnp.bfloat16)
    low = (value - high.astype(jnp.float32)).astype(jnp.bfloat16)
    return high, low


def look_up(table, index):
    row, lane = index // LANES, index % LANES
    found = jnp.zeros(index.shape, table.dtype)
    for t in range(table.shape[0]):
        spread = jnp.broadcast_to(table[t : t + 1, :], index.shape)
        here = jnp.take_along_axis(spread, lane, axis=1, mode="promise_in_bounds")
        found = jnp.where(row == t, here, found)
    return found


def kernel(
    n_row, n_col,
    lam_hbm, inter_hbm, exch_hbm, occ_hbm, virt_hbm, rows_hbm, cols_hbm, anti_ref, denom_ref,
    lam, inter, acc, stage, recv, summed, whole, cyc, exch, occ, virt, rows, cols, pair,
    small_sem, own_sem, inter_sem, near_send, near_recv, far_send, far_recv, relay_send, relay_recv,
    tile_send, tile_recv, row_send, row_recv,
):
    n_dev = n_row * n_col
    my_row, my_col = lax.axis_index("row"), lax.axis_index("col")
    me = my_row * n_col + my_col
    held, depth = lam_hbm.shape
    step = depth // CHUNKS
    width = inter_hbm.shape[1]
    bra = lam.shape[0]
    blocks = width // LANES

    def inter_copy(k):
        return pltpu.make_async_copy(
            inter_hbm.at[pl.ds(pl.multiple_of(k * step, step), step), :], inter.at[k], inter_sem.at[k]
        )

    for k in range(CHUNKS):
        inter_copy(k).start()

    barrier = pltpu.get_barrier_semaphore()

    def greet_row(k, carry):
        pl.semaphore_signal(
            barrier, inc=1, device_id=(lax.rem(my_row + k, n_row), my_col), device_id_type=MESH
        )
        return carry

    for d in range(1, n_col):
        pl.semaphore_signal(
            barrier, inc=1, device_id=(my_row, lax.rem(my_col + d, n_col)), device_id_type=MESH
        )
    lax.fori_loop(1, n_row, greet_row, 0)

    my_rows = pl.ds(pl.multiple_of(my_col * held, held), held)
    own = pltpu.make_async_copy(lam_hbm, lam.at[my_rows, :], own_sem)
    own.start()
    small = [
        pltpu.make_async_copy(src, dst, small_sem.at[s])
        for s, (src, dst) in enumerate(
            [(exch_hbm, exch), (occ_hbm, occ), (virt_hbm, virt), (rows_hbm, rows), (cols_hbm, cols)]
        )
    ]
    for copy in small:
        copy.start()
    pl.semaphore_wait(barrier, n_row + n_col - 2)

    def chunk(k):
        return pl.ds(pl.multiple_of(k * step, step), step)

    def rows_of(col):
        return pl.ds(pl.multiple_of(col * held, held), held)

    core = lax.rem(my_col, 2)
    mate = my_col + 1 - 2 * core
    n_far = n_col // 2 - 1
    peers = [lax.rem(my_col + 2 * d, n_col) for d in range(1, n_far + 1)]

    def push(k, carry):
        for peer in peers:
            pltpu.make_async_remote_copy(
                src_ref=lam_hbm.at[:, chunk(k)],
                dst_ref=lam.at[my_rows, chunk(k)],
                send_sem=far_send,
                recv_sem=far_recv.at[k],
                device_id=(my_row, peer),
                device_id_type=MESH,
            ).start()
        return carry

    def forward(k):
        arrived = lam.at[pl.ds(0, n_far * held), chunk(k)]
        pltpu.make_async_copy(arrived, arrived, far_recv.at[k]).wait()
        for peer in peers:
            pltpu.make_async_remote_copy(
                src_ref=lam.at[rows_of(peer), chunk(k)],
                dst_ref=lam.at[rows_of(peer), chunk(k)],
                send_sem=relay_send,
                recv_sem=relay_recv.at[k],
                device_id=(my_row, mate),
                device_id_type=MESH,
            ).start()

    lax.fori_loop(0, CHUNKS, push, 0)
    near = pltpu.make_async_remote_copy(
        src_ref=lam_hbm,
        dst_ref=lam.at[my_rows, :],
        send_sem=near_send,
        recv_sem=near_recv,
        device_id=(my_row, mate),
        device_id_type=MESH,
    )
    near.start()
    for k in range(AHEAD):
        forward(k)
    near.wait_recv()
    own.wait()
    acc[...] = jnp.zeros_like(acc)

    def multiply(k, carry):
        @pl.when(k + AHEAD < CHUNKS)
        def _():
            forward(k + AHEAD)

        arrived = lam.at[pl.ds(0, n_far * held), chunk(k)]
        pltpu.make_async_copy(arrived, arrived, relay_recv.at[k]).wait()
        inter_copy(k).wait()
        high, low = split(lam[:, chunk(k)])
        both = jnp.concatenate([high, low], axis=0)
        for c in range(0, width, TILE):
            at = slice(c, c + TILE)
            first = second = 0.0
            for r in range(0, step, TILE):
                rows_at = slice(r, r + TILE)
                inter_high, inter_low = split(inter[k, rows_at, at])
                first += jnp.dot(both[:, rows_at], inter_high, preferred_element_type=jnp.float32)
                second += jnp.dot(high[:, rows_at], inter_low, preferred_element_type=jnp.float32)
            acc[:, at] += first[:bra] + (first[bra:] + second)
        return carry

    lax.fori_loop(0, CHUNKS, multiply, 0)

    for b in range(blocks):
        stage[:, b, :] = acc[:, b * LANES : (b + 1) * LANES]

    def group(row):
        return pl.ds(row * n_col, n_col)

    def scatter(k, carry):
        to = lax.rem(my_row + k, n_row)
        pltpu.make_async_remote_copy(
            src_ref=stage.at[group(to)],
            dst_ref=recv.at[group(my_row)],
            send_sem=tile_send,
            recv_sem=tile_recv,
            device_id=(to, my_col),
            device_id_type=MESH,
        ).start()
        return carry

    lax.fori_loop(1, n_row, scatter, 0)
    recv[group(my_row)] = stage[group(my_row)]

    for copy in small:
        copy.wait()
    lines = cyc.shape[0]
    for q in range(lines):
        for s in range(2):
            pair[s, q : q + 1, :] = cols[s : s + 1, q * LANES : (q + 1) * LANES]
    col_part = look_up(virt[...], pair[0]) + look_up(virt[...], pair[1])
    orbital = jnp.sum(
        jnp.where(lax.broadcasted_iota(jnp.int32, rows.shape, 1) == me, rows[...], 0), axis=1, keepdims=True
    )
    spread = (2, occ.shape[1])
    picked = jnp.sum(
        jnp.where(
            lax.broadcasted_iota(jnp.int32, spread, 1) == orbital, jnp.broadcast_to(occ[...], spread), 0.0
        ),
        axis=1,
        keepdims=True,
    )
    row_part = picked[0:1] + picked[1:2]
    denom_ref[...] = row_part - col_part
    index = exch[...]

    rest = recv.at[pl.ds(0, n_dev - n_col)]
    pltpu.make_async_copy(rest, rest, tile_recv).wait()
    total = recv[pl.ds(0, n_col)]
    for i in range(1, n_row):
        total = total + recv[pl.ds(i * n_col, n_col)]
    summed[...] = total

    for d in range(1, n_col):
        to = lax.rem(my_col + d, n_col)
        pltpu.make_async_remote_copy(
            src_ref=summed.at[to],
            dst_ref=whole.at[my_col],
            send_sem=row_send,
            recv_sem=row_recv,
            device_id=(my_row, to),
            device_id_type=MESH,
        ).start()
    whole[my_col] = summed[my_col]
    rest = whole.at[pl.ds(0, n_col - 1)]
    pltpu.make_async_copy(rest, rest, row_recv).wait()
    for j in range(n_col):
        cyc[j * blocks : (j + 1) * blocks, :] = whole[j]
    cycle = cyc[...]
    anti_ref[...] = cycle - look_up(cycle, index)

    sent = stage.at[pl.ds(0, n_dev - n_col)]
    pltpu.make_async_copy(sent, sent, tile_send).wait()
    sent = summed.at[pl.ds(0, n_col - 1)]
    pltpu.make_async_copy(sent, sent, row_send).wait()
    near.wait_send()
    gone = lam.at[pl.ds(0, n_far * held), :]
    pltpu.make_async_copy(gone, gone, far_send).wait()
    pltpu.make_async_copy(gone, gone, relay_send).wait()


def shards(
    lambda_amps, cycle_inter, exchanged, occ_energy, virt_energy, row_orbitals, col_orbitals
):
    n_row, n_col = lax.axis_size("row"), lax.axis_size("col")
    n_dev = n_row * n_col
    held, depth = lambda_amps.shape
    width = cycle_inter.shape[1]
    bra = held * n_col
    window = exchanged.shape[0]
    assert bra == n_dev and n_col % 2 == 0 and n_col > 2
    blocks, lines = width // LANES, window // LANES
    f32, i32 = jnp.float32, jnp.int32
    small = [
        exchanged.reshape(lines, LANES),
        occ_energy.reshape(1, -1),
        virt_energy.reshape(-1, LANES),
        row_orbitals.T,
        col_orbitals.T,
    ]
    line = jax.ShapeDtypeStruct((lines, LANES), f32)
    anti, denom = pl.pallas_call(
        functools.partial(kernel, n_row, n_col),
        out_shape=(line, line),
        in_specs=[pl.BlockSpec(memory_space=pl.ANY)] * 7,
        out_specs=(pl.BlockSpec(memory_space=pltpu.VMEM),) * 2,
        scratch_shapes=[
            pltpu.VMEM((bra, depth), f32),
            pltpu.VMEM((CHUNKS, depth // CHUNKS, width), f32),
            pltpu.VMEM((bra, width), f32),
            pltpu.VMEM((n_dev, blocks, LANES), f32),
            pltpu.VMEM((n_dev, blocks, LANES), f32),
            pltpu.VMEM((n_col, blocks, LANES), f32),
            pltpu.VMEM((n_col, blocks, LANES), f32),
            pltpu.VMEM((lines, LANES), f32),
            *[pltpu.VMEM(x.shape, x.dtype) for x in small],
            pltpu.VMEM((2, lines, LANES), i32),
            pltpu.SemaphoreType.DMA((5,)),
            pltpu.SemaphoreType.DMA,
            pltpu.SemaphoreType.DMA((CHUNKS,)),
            pltpu.SemaphoreType.DMA,
            pltpu.SemaphoreType.DMA,
            pltpu.SemaphoreType.DMA,
            pltpu.SemaphoreType.DMA((CHUNKS,)),
            pltpu.SemaphoreType.DMA,
            pltpu.SemaphoreType.DMA((CHUNKS,)),
            pltpu.SemaphoreType.DMA,
            pltpu.SemaphoreType.DMA,
            pltpu.SemaphoreType.DMA,
            pltpu.SemaphoreType.DMA,
        ],
        compiler_params=pltpu.CompilerParams(
            collective_id=0, has_side_effects=True, vmem_limit_bytes=56 * 2**20
        ),
        cost_estimate=pl.CostEstimate(
            flops=2 * bra * depth * width, bytes_accessed=4 * depth * width, transcendentals=0
        ),
    )(lambda_amps, cycle_inter, *small)
    return (anti / denom).reshape(1, window)


def solution(mesh):
    placed = (P("col", "row"), P("row", "col"), P(), P(), P(), P(), P())
    return jax.shard_map(
        shards, mesh=mesh, in_specs=placed, out_specs=P(("row", "col"), None), check_vma=False
    )
```

```python
import functools

import jax
import jax.numpy as jnp
from jax import lax
from jax.experimental import pallas as pl
from jax.experimental.pallas import tpu as pltpu
from jax.sharding import PartitionSpec as P

MESH = pl.DeviceIdType.MESH
LANES = 128
CHUNKS = 4
AHEAD = 1
TILE = 256


def split(value):
    high = value.astype(jnp.bfloat16)
    low = (value - high.astype(jnp.float32)).astype(jnp.bfloat16)
    return high, low


def look_up(table, index):
    row, lane = index // LANES, index % LANES
    found = jnp.zeros(index.shape, table.dtype)
    for t in range(table.shape[0]):
        spread = jnp.broadcast_to(table[t : t + 1, :], index.shape)
        here = jnp.take_along_axis(spread, lane, axis=1, mode="promise_in_bounds")
        found = jnp.where(row == t, here, found)
    return found


def kernel(
    n_row, n_col,
    lam_hbm, inter_hbm, exch_hbm, occ_hbm, virt_hbm, rows_hbm, cols_hbm, anti_ref, denom_ref,
    lam, inter, acc, stage, recv, cyc, exch, occ, virt, rows, cols, pair,
    small_sem, own_sem, inter_sem, near_send, near_recv, far_send, far_recv, relay_send, relay_recv,
    tile_send, tile_recv,
):
    n_dev = n_row * n_col
    my_row, my_col = lax.axis_index("row"), lax.axis_index("col")
    me = my_row * n_col + my_col
    held, depth = lam_hbm.shape
    step = depth // CHUNKS
    width = inter_hbm.shape[1]
    bra = lam.shape[0]
    blocks = width // LANES

    def chunk(k):
        return pl.ds(k * step if isinstance(k, int) else pl.multiple_of(k * step, step), step)

    def inter_copy(k):
        return pltpu.make_async_copy(
            inter_hbm.at[chunk(k), :], inter.at[k], inter_sem.at[k]
        )

    barrier = pltpu.get_barrier_semaphore()

    columns = [my_col] + [lax.rem(my_col + d, n_col) for d in range(1, n_col)]

    def greet(row, cols_of):
        for col in cols_of:
            pl.semaphore_signal(barrier, inc=1, device_id=(row, col), device_id_type=MESH)

    def greet_row(k, carry):
        greet(lax.rem(my_row + k, n_row), columns)
        return carry

    lax.fori_loop(1, n_row, greet_row, 0)
    greet(my_row, columns[1:])

    for k in range(CHUNKS):
        inter_copy(k).start()

    my_rows = pl.ds(pl.multiple_of(my_col * held, held), held)
    own = pltpu.make_async_copy(lam_hbm, lam.at[my_rows, :], own_sem)
    own.start()
    small = [
        pltpu.make_async_copy(src, dst, small_sem.at[s])
        for s, (src, dst) in enumerate(
            [(exch_hbm, exch), (occ_hbm, occ), (virt_hbm, virt), (rows_hbm, rows), (cols_hbm, cols)]
        )
    ]
    for copy in small:
        copy.start()
    pl.semaphore_wait(barrier, n_dev - 1)

    def rows_of(col):
        return pl.ds(pl.multiple_of(col * held, held), held)

    core = lax.rem(my_col, 2)
    mate = my_col + 1 - 2 * core
    n_far = n_col // 2 - 1
    peers = [lax.rem(my_col + 2 * d, n_col) for d in range(1, n_far + 1)]

    def push(k):
        for peer in peers:
            pltpu.make_async_remote_copy(
                src_ref=lam_hbm.at[:, chunk(k)],
                dst_ref=lam.at[my_rows, chunk(k)],
                send_sem=far_send,
                recv_sem=far_recv.at[k],
                device_id=(my_row, peer),
                device_id_type=MESH,
            ).start()

    def forward(k):
        arrived = lam.at[pl.ds(0, n_far * held), chunk(k)]
        pltpu.make_async_copy(arrived, arrived, far_recv.at[k]).wait()
        for peer in peers:
            pltpu.make_async_remote_copy(
                src_ref=lam.at[rows_of(peer), chunk(k)],
                dst_ref=lam.at[rows_of(peer), chunk(k)],
                send_sem=relay_send,
                recv_sem=relay_recv.at[k],
                device_id=(my_row, mate),
                device_id_type=MESH,
            ).start()

    for k in range(CHUNKS):
        push(k)
    near = pltpu.make_async_remote_copy(
        src_ref=lam_hbm,
        dst_ref=lam.at[my_rows, :],
        send_sem=near_send,
        recv_sem=near_recv,
        device_id=(my_row, mate),
        device_id_type=MESH,
    )
    near.start()
    for k in range(AHEAD):
        forward(k)
    near.wait_recv()
    own.wait()
    acc[...] = jnp.zeros_like(acc)

    def multiply(k, carry):
        @pl.when(k + AHEAD < CHUNKS)
        def _():
            forward(k + AHEAD)

        arrived = lam.at[pl.ds(0, n_far * held), chunk(k)]
        pltpu.make_async_copy(arrived, arrived, relay_recv.at[k]).wait()
        inter_copy(k).wait()
        high, low = split(lam[:, chunk(k)])
        both = jnp.concatenate([high, low], axis=0)
        for c in range(0, width, TILE):
            at = slice(c, c + TILE)
            first = second = 0.0
            for r in range(0, step, TILE):
                rows_at = slice(r, r + TILE)
                inter_high, inter_low = split(inter[k, rows_at, at])
                first += jnp.dot(both[:, rows_at], inter_high, preferred_element_type=jnp.float32)
                second += jnp.dot(high[:, rows_at], inter_low, preferred_element_type=jnp.float32)
            acc[:, at] += first[:bra] + (first[bra:] + second)
        return carry

    lax.fori_loop(0, CHUNKS, multiply, 0)

    for b in range(blocks):
        stage[:, b, :] = acc[:, b * LANES : (b + 1) * LANES]

    def scatter(row, cols_of):
        for col in cols_of:
            pltpu.make_async_remote_copy(
                src_ref=stage.at[row * n_col + col],
                dst_ref=recv.at[me],
                send_sem=tile_send,
                recv_sem=tile_recv,
                device_id=(row, col),
                device_id_type=MESH,
            ).start()

    def scatter_row(k, carry):
        scatter(lax.rem(my_row + k, n_row), columns)
        return carry

    lax.fori_loop(1, n_row, scatter_row, 0)
    scatter(my_row, columns[1:])
    recv[me] = stage[me]

    for copy in small:
        copy.wait()
    lines = cyc.shape[0]
    for q in range(lines):
        for s in range(2):
            pair[s, q : q + 1, :] = cols[s : s + 1, q * LANES : (q + 1) * LANES]
    col_part = look_up(virt[...], pair[0]) + look_up(virt[...], pair[1])
    orbital = jnp.sum(
        jnp.where(lax.broadcasted_iota(jnp.int32, rows.shape, 1) == me, rows[...], 0), axis=1, keepdims=True
    )
    spread = (2, occ.shape[1])
    picked = jnp.sum(
        jnp.where(
            lax.broadcasted_iota(jnp.int32, spread, 1) == orbital, jnp.broadcast_to(occ[...], spread), 0.0
        ),
        axis=1,
        keepdims=True,
    )
    row_part = picked[0:1] + picked[1:2]
    denom_ref[...] = row_part - col_part
    index = exch[...]

    rest = recv.at[pl.ds(0, n_dev - 1)]
    pltpu.make_async_copy(rest, rest, tile_recv).wait()
    total = recv[pl.ds(0, n_col)]
    for i in range(1, n_row):
        total = total + recv[pl.ds(i * n_col, n_col)]
    for j in range(n_col):
        cyc[j * blocks : (j + 1) * blocks, :] = total[j]
    cycle = cyc[...]
    anti_ref[...] = cycle - look_up(cycle, index)

    sent = stage.at[pl.ds(0, n_dev - 1)]
    pltpu.make_async_copy(sent, sent, tile_send).wait()
    near.wait_send()
    gone = lam.at[pl.ds(0, n_far * held), :]
    pltpu.make_async_copy(gone, gone, far_send).wait()
    pltpu.make_async_copy(gone, gone, relay_send).wait()


def shards(
    lambda_amps, cycle_inter, exchanged, occ_energy, virt_energy, row_orbitals, col_orbitals
):
    n_row, n_col = lax.axis_size("row"), lax.axis_size("col")
    n_dev = n_row * n_col
    held, depth = lambda_amps.shape
    width = cycle_inter.shape[1]
    bra = held * n_col
    window = exchanged.shape[0]
    assert bra == n_dev and n_col % 2 == 0 and n_col > 2
    blocks, lines = width // LANES, window // LANES
    f32, i32 = jnp.float32, jnp.int32
    small = [
        exchanged.reshape(lines, LANES),
        occ_energy.reshape(1, -1),
        virt_energy.reshape(-1, LANES),
        row_orbitals.T,
        col_orbitals.T,
    ]
    line = jax.ShapeDtypeStruct((lines, LANES), f32)
    anti, denom = pl.pallas_call(
        functools.partial(kernel, n_row, n_col),
        out_shape=(line, line),
        in_specs=[pl.BlockSpec(memory_space=pl.ANY)] * 7,
        out_specs=(pl.BlockSpec(memory_space=pltpu.VMEM),) * 2,
        scratch_shapes=[
            pltpu.VMEM((bra, depth), f32),
            pltpu.VMEM((CHUNKS, depth // CHUNKS, width), f32),
            pltpu.VMEM((bra, width), f32),
            pltpu.VMEM((n_dev, blocks, LANES), f32),
            pltpu.VMEM((n_dev, blocks, LANES), f32),
            pltpu.VMEM((lines, LANES), f32),
            *[pltpu.VMEM(x.shape, x.dtype) for x in small],
            pltpu.VMEM((2, lines, LANES), i32),
            pltpu.SemaphoreType.DMA((5,)),
            pltpu.SemaphoreType.DMA,
            pltpu.SemaphoreType.DMA((CHUNKS,)),
            pltpu.SemaphoreType.DMA,
            pltpu.SemaphoreType.DMA,
            pltpu.SemaphoreType.DMA,
            pltpu.SemaphoreType.DMA((CHUNKS,)),
            pltpu.SemaphoreType.DMA,
            pltpu.SemaphoreType.DMA((CHUNKS,)),
            pltpu.SemaphoreType.DMA,
            pltpu.SemaphoreType.DMA,
        ],
        compiler_params=pltpu.CompilerParams(
            collective_id=0, has_side_effects=True, vmem_limit_bytes=56 * 2**20
        ),
        cost_estimate=pl.CostEstimate(
            flops=2 * bra * depth * width, bytes_accessed=4 * depth * width, transcendentals=0
        ),
    )(lambda_amps, cycle_inter, *small)
    return (anti / denom).reshape(1, window)


def solution(mesh):
    placed = (P("col", "row"), P("row", "col"), P(), P(), P(), P(), P())
    return jax.shard_map(
        shards, mesh=mesh, in_specs=placed, out_specs=P(("row", "col"), None), check_vma=False
    )
```
